32 devices in a mesh: rep: 2 (over y), ad: 4 (over z), tp: 4 (over x, core).
Axes of the slice: x: 2, y: 2, z: 4, core: 2. Of those that a mesh axis runs over, the one named last changes fastest.
Arguments:
- tokens: bfloat16 [2048, 8192], P(('rep', 'ad'), 'tp'), parts along dimension 0, may hold values from -6 to 6
- request_adapter: int32 [2048], P(('rep', 'ad')), parts along dimension 0, may hold values from 0 to 31, as said below
- adapter_page_lookup: int32 [64], P('rep'), parts along dimension 0, may hold values from 0 to 31, as said below
- base_key_value_weight: bfloat16 [8192, 2048], P(None, 'tp'), may hold values from -0.0625 to 0.0625
- down_factor_pages: bfloat16 [64, 8192, 64], P(('rep', 'ad'), 'tp'), parts along dimension 0, may hold values from -0.0625 to 0.0625
- up_factor_pages: bfloat16 [64, 64, 2048], P(('rep', 'ad'), None, 'tp'), parts along dimension 0, may hold values from -0.75 to 0.75
Outputs:
- kv_out: bfloat16 [2048, 2048], P(('rep', 'ad'), 'tp'), parts along dimension 0
The draws below stay inside these ranges and needn't reach their ends.
There are 2 independent parts, one for each index of `rep`. The reference program is written for one: setup_inputs(seed, part) draws one part's arguments, and reference() takes and returns one part's arrays. A program takes and returns all parts, laid end to end along the dimension named above; an argument that names none is the same for every part. Nothing has to cross between parts.
Inputs may be any that keep to these rules, and one draw needn't show every extreme that they name: `request_adapter`: within each aligned block of 256 requests, at most 128 requests name adapters whose pages lie in one aligned block of 8 pages; one block of pages receives exactly 128 requests from every block of requests. `adapter_page_lookup`: A permutation.
All inputs are finite; a program needn't handle non-finite values.
Results may differ from the reference program's by a relative error of at most 0.0049.
Values may be sent and summed in bfloat16 or wider, within the bound.
A program may use at most 64 MiB of HBM per device.

```python
import jax
import jax.numpy as jnp
from jax import lax

MODEL_WIDTH = 8192
KEY_VALUE_WIDTH = 2048
ADAPTER_RANK = 64
TOK_DEV = 256
ADAPT_DEV = 8
OWNERS = 4
ADAPTER_PAGES = 32
TOKENS = 1024
CAP = 128


def route_tables(key):
    adapter_page_lookup = jax.random.permutation(jax.random.fold_in(key, 11), ADAPTER_PAGES).astype(jnp.int32)
    adapter_at = jnp.zeros((ADAPTER_PAGES,), jnp.int32).at[adapter_page_lookup].set(jnp.arange(ADAPTER_PAGES, dtype=jnp.int32))
    hotter = jax.random.randint(jax.random.fold_in(key, 12), (), 0, OWNERS).astype(jnp.int32)
    scores = jax.random.randint(jax.random.fold_in(key, 13), (OWNERS, TOK_DEV), 0, 1 << 20).astype(jnp.int32)
    scores = scores * TOK_DEV + jnp.arange(TOK_DEV, dtype=jnp.int32)[None, :]
    order = jnp.argsort(scores, axis=1).astype(jnp.int32)
    offset = jax.random.randint(jax.random.fold_in(key, 14), (OWNERS, 1), 0, OWNERS).astype(jnp.int32)
    others = (order - CAP + offset) % max(OWNERS - 1, 1)
    target = jnp.where(order < CAP, hotter, (hotter + 1 + others) % OWNERS)
    within = jax.random.randint(jax.random.fold_in(key, 15), (OWNERS, TOK_DEV), 0, ADAPT_DEV).astype(jnp.int32)
    request_adapter = adapter_at[(target * ADAPT_DEV + within).reshape(-1)]
    return (adapter_page_lookup, request_adapter.astype(jnp.int32))


def draw_request_adapter(key, part):
    return route_tables(key)[1]


def draw_adapter_page_lookup(key, part):
    return route_tables(key)[0]


def block_scale(own_key, dims, pieces, low, top_value):
    level, own = 1.0, jax.random.fold_in(own_key, 6)
    for dim, shards_of in pieces:
        heights = jnp.exp(jax.random.uniform(jax.random.fold_in(own, dim), (shards_of,), jnp.float32, low / len(pieces), top_value / len(pieces)))
        level = level * jnp.repeat(heights, dims[dim] // shards_of).reshape([-1 if axis == dim else 1 for axis in range(len(dims))])
    return level


def bell_draw(stream_key, shape, spread, reach, split=(), kind=jnp.bfloat16):
    result = jax.random.normal(stream_key, shape, jnp.float32) * spread
    if len(split) > 0:
        result = block_scale(stream_key, shape, split, -0.22, 0.18) * result
    return jnp.clip(result, min=-reach, max=reach).astype(kind)


def setup_inputs(seed: int = 0, part: int = 0) -> dict:
    key_of = jax.random.split(jax.random.key(seed), 7)
    part_keys = jax.random.split(jax.random.fold_in(key_of[6], part), 7)
    return {
        "tokens": bell_draw(part_keys[0], (TOKENS, MODEL_WIDTH), 1.0, 6.0, ((0, 4), (1, 4))),
        "request_adapter": draw_request_adapter(jax.random.fold_in(jax.random.fold_in(key_of[6], part), 71), part),
        "adapter_page_lookup": draw_adapter_page_lookup(jax.random.fold_in(jax.random.fold_in(key_of[6], part), 71), part),
        "base_key_value_weight": bell_draw(key_of[3], (MODEL_WIDTH, KEY_VALUE_WIDTH), MODEL_WIDTH ** -0.5, 0.0625, ((1, 4),)),
        "down_factor_pages": bell_draw(part_keys[4], (ADAPTER_PAGES, MODEL_WIDTH, ADAPTER_RANK), MODEL_WIDTH ** -0.5, 0.0625, ((0, 4), (1, 4))),
        "up_factor_pages": bell_draw(part_keys[5], (ADAPTER_PAGES, ADAPTER_RANK, KEY_VALUE_WIDTH), ADAPTER_RANK ** -0.5, 0.75, ((0, 4), (2, 4))),
    }


def adapter_slab(arguments):
    token_rows, page_entries, down_factor_pages, up_factor_pages = arguments
    first_factor = down_factor_pages[page_entries].astype(jnp.float32)
    shrink = jnp.einsum("bd,bdr->br", token_rows.astype(jnp.float32), first_factor).astype(jnp.bfloat16)
    second_factor = up_factor_pages[page_entries].astype(jnp.float32)
    return jnp.einsum("br,bre->be", shrink.astype(jnp.float32), second_factor).astype(jnp.bfloat16)


def reference(tokens, request_adapter, adapter_page_lookup, base_key_value_weight, down_factor_pages, up_factor_pages):
    base = jnp.dot(tokens, base_key_value_weight, preferred_element_type=jnp.float32)
    page = adapter_page_lookup[request_adapter].astype(jnp.int32)
    blocks = TOKENS // 32
    token_rows = tokens.reshape(blocks, 32, MODEL_WIDTH)
    page_entries = page.reshape(blocks, 32)

    def one_block(arguments):
        return adapter_slab((arguments[0], arguments[1], down_factor_pages, up_factor_pages))

    adapter_update = lax.map(one_block, (token_rows, page_entries)).reshape(TOKENS, KEY_VALUE_WIDTH)
    return (base + adapter_update.astype(jnp.float32)).astype(jnp.bfloat16)
```

```python
import functools

import jax
import jax.numpy as jnp
from jax import lax
from jax.experimental import pallas as pl
from jax.experimental.pallas import tpu as pltpu
from jax.sharding import PartitionSpec as P

MESH = pl.DeviceIdType.MESH
LANES = 128
DEPTH = 512


def kernel(
    n, rank, send_ref, which_ref, tok_ref, comb_ref, up_ref, w_hbm, down_hbm, out_ref,
    recv, rwhich, gath, w, down, dcat, acc, part, dsend, ret,
    local_sem, row_send, row_recv, which_send, which_recv,
    tok_send, tok_recv, part_send, part_recv, ret_send, ret_recv,
):
    me, t = lax.axis_index("ad"), lax.axis_index("tp")
    sibling = t + 1 - 2 * lax.rem(t, 2)
    across = lax.rem(t + 2, 4)
    diagonal = lax.rem(sibling + 2, 4)
    cap, wide = send_ref.shape[1], dcat.shape[1]
    width = tok_ref.shape[1]

    barrier = pltpu.get_barrier_semaphore()

    @pl.loop(1, n)
    def _(s):
        pl.semaphore_signal(barrier, inc=1, device_id={"ad": lax.rem(me + s, n)}, device_id_type=MESH)

    for s in range(1, 4):
        pl.semaphore_signal(barrier, inc=1, device_id={"tp": lax.rem(t + s, 4)}, device_id_type=MESH)
    down_copy = pltpu.make_async_copy(down_hbm, down, local_sem.at[0])
    w_copy = pltpu.make_async_copy(w_hbm, w, local_sem.at[1])
    down_copy.start()
    w_copy.start()
    pl.semaphore_wait(barrier, n - 1 + 3)

    def rows_to(j):
        return pltpu.make_async_remote_copy(
            src_ref=send_ref.at[j], dst_ref=recv.at[me], send_sem=row_send.at[j],
            recv_sem=row_recv.at[me], device_id={"ad": j}, device_id_type=MESH)

    def rows_from(j):
        return pltpu.make_async_remote_copy(
            src_ref=send_ref.at[j], dst_ref=recv.at[j], send_sem=row_send.at[j],
            recv_sem=row_recv.at[j], device_id={"ad": j}, device_id_type=MESH)

    def which_copy(j, slot):
        return pltpu.make_async_remote_copy(
            src_ref=which_ref.at[j], dst_ref=rwhich.at[slot], send_sem=which_send.at[j],
            recv_sem=which_recv.at[slot], device_id={"ad": j}, device_id_type=MESH)

    def token_copy(k, src, slot, to):
        return pltpu.make_async_remote_copy(
            src_ref=src, dst_ref=gath.at[slot], send_sem=tok_send.at[k],
            recv_sem=tok_recv.at[k], device_id={"tp": to}, device_id_type=MESH)

    def part_copy(k, j, slot):
        return pltpu.make_async_remote_copy(
            src_ref=part.at[t, j], dst_ref=part.at[slot, j], send_sem=part_send.at[k, j],
            recv_sem=part_recv.at[slot, j], device_id={"tp": lax.rem(t + k, 4)}, device_id_type=MESH)

    def part_from(k, j):
        slot = lax.rem(t + 4 - k, 4)
        return pltpu.make_async_remote_copy(
            src_ref=part.at[t, j], dst_ref=part.at[slot, j], send_sem=part_send.at[k, j],
            recv_sem=part_recv.at[slot, j], device_id={"tp": slot}, device_id_type=MESH)

    def ret_copy(j, slot):
        return pltpu.make_async_remote_copy(
            src_ref=dsend.at[j], dst_ref=ret.at[slot], send_sem=ret_send.at[j],
            recv_sem=ret_recv.at[slot], device_id={"ad": j}, device_id_type=MESH)

    @pl.loop(1, n)
    def _(s):
        j = lax.rem(me + s, n)
        which_copy(j, me).start()
        rows_to(j).start()

    token_copy(1, tok_ref, t, across).start()
    token_copy(0, tok_ref, t, sibling).start()

    down_copy.wait()
    for e in range(down.shape[0]):
        dcat[:, e * rank : (e + 1) * rank] = down[e]

    lane_page = (lax.broadcasted_iota(jnp.int32, (cap, wide), 1) // rank).astype(jnp.float32)
    same = lax.broadcasted_iota(jnp.int32, (cap, cap), 0) == lax.broadcasted_iota(jnp.int32, (cap, cap), 1)

    def page_mask(tile):
        line = jnp.broadcast_to(tile[0:1, :].astype(jnp.float32), (cap, cap))
        spread = jnp.where(same, line, 0.0).astype(jnp.bfloat16)
        column = jnp.dot(spread, jnp.ones((cap, wide), jnp.bfloat16), preferred_element_type=jnp.float32)
        return column == lane_page

    def partial(rows, tile, j):
        first = jnp.dot(rows, dcat[...], preferred_element_type=jnp.float32)
        first = jnp.where(page_mask(tile), first, 0.0)
        total = first[:, :LANES]
        for k in range(1, wide // LANES):
            total = total + first[:, k * LANES : (k + 1) * LANES]
        part[t, j] = total
        for k in range(1, 4):
            part_copy(k, j, t).start()

    def update(tile, j):
        for k in range(1, 4):
            part_from(k, j).wait_recv()
        shrink = part[0, j] + part[1, j] + part[2, j] + part[3, j]
        spread = jnp.concatenate([shrink] * (wide // LANES), axis=1)
        spread = jnp.where(page_mask(tile), spread, 0.0).astype(jnp.bfloat16)
        return jnp.dot(spread, up_ref[...], preferred_element_type=jnp.float32).astype(jnp.bfloat16)

    partial(send_ref[me], which_ref[me], me)

    acc[...] = jnp.zeros_like(acc)
    w_copy.wait()

    def add_base(block, owner):
        @pl.loop(0, width // DEPTH)
        def _(i):
            at = pl.multiple_of(i * DEPTH, DEPTH)
            row = pl.multiple_of(owner * width + i * DEPTH, DEPTH)
            acc[...] += jnp.dot(
                block[:, pl.ds(at, DEPTH)], w[pl.ds(row, DEPTH), :], preferred_element_type=jnp.float32)

    add_base(tok_ref, t)
    token_copy(0, tok_ref, sibling, sibling).wait_recv()
    add_base(gath.at[sibling], sibling)
    token_copy(1, tok_ref, across, across).wait_recv()
    token_copy(2, gath.at[across], across, sibling).start()
    add_base(gath.at[across], across)
    token_copy(2, gath.at[across], diagonal, sibling).wait_recv()
    add_base(gath.at[diagonal], diagonal)
    ret[me] = update(which_ref[me], me)

    @pl.loop(1, n)
    def _(s):
        j = lax.rem(me + s, n)
        which_copy(j, j).wait_recv()
        rows_from(j).wait_recv()
        partial(recv[j], rwhich[j], j)

    @pl.loop(1, n)
    def _(s):
        j = lax.rem(me + s, n)
        dsend[j] = update(rwhich[j], j)
        ret_copy(j, me).start()

    @pl.loop(1, n)
    def _(s):
        j = lax.rem(me + s, n)
        ret_copy(j, j).wait_recv()

    back = ret[...].reshape(n * cap, out_ref.shape[1])
    change = jnp.dot(comb_ref[...], back, preferred_element_type=jnp.float32)
    out_ref[...] = (acc[...] + change).astype(out_ref.dtype)

    @pl.loop(1, n)
    def _(s):
        j = lax.rem(me + s, n)
        which_copy(j, me).wait_send()
        rows_to(j).wait_send()
        ret_copy(j, me).wait_send()

    @pl.loop(0, n)
    def _(j):
        for k in range(1, 4):
            part_copy(k, j, t).wait_send()

    token_copy(0, tok_ref, t, sibling).wait_send()
    token_copy(1, tok_ref, t, across).wait_send()
    token_copy(2, gath.at[across], across, sibling).wait_send()


def shards(
    tokens,
    request_adapter,
    adapter_page_lookup,
    base_key_value_weight,
    down_factor_pages,
    up_factor_pages,
):
    n = lax.axis_size("ad")
    token_rows, width = tokens.shape
    pages, _, rank = down_factor_pages.shape
    columns = base_key_value_weight.shape[1]
    wide = pages * rank
    cap = max(16, min(4 * token_rows // n, token_rows // 2))
    slots = n * cap

    catalog = jnp.arange(adapter_page_lookup.shape[0], dtype=jnp.int32)
    matches = request_adapter[:, None] == catalog[None, :]
    page = jnp.sum(jnp.where(matches, adapter_page_lookup[None, :], 0), axis=1)
    target = page // pages
    within = page % pages
    order = jnp.arange(token_rows, dtype=jnp.int32)
    earlier = (target[:, None] == target[None, :]) & (order[None, :] < order[:, None])
    position = jnp.sum(earlier.astype(jnp.int32), axis=1)
    place = target * cap + position
    slot = jnp.arange(slots, dtype=jnp.int32)
    dispatch = slot[:, None] == place[None, :]
    combine = (place[:, None] == slot[None, :]).astype(jnp.bfloat16)
    send = jnp.dot(
        dispatch.astype(jnp.bfloat16), tokens, preferred_element_type=jnp.float32
    ).astype(jnp.bfloat16).reshape(n, cap, width)
    which = jnp.sum(jnp.where(dispatch, within[None, :], 0), axis=1).astype(jnp.bfloat16)
    which = jnp.broadcast_to(which.reshape(n, 1, cap), (n, 16, cap))

    vmem = pl.BlockSpec(memory_space=pltpu.VMEM)
    hbm = pl.BlockSpec(memory_space=pl.ANY)
    bf16, f32 = jnp.bfloat16, jnp.float32
    dma = pltpu.SemaphoreType.DMA
    return pl.pallas_call(
        functools.partial(kernel, n, rank),
        out_shape=jax.ShapeDtypeStruct((token_rows, columns), bf16),
        in_specs=[vmem] * 5 + [hbm] * 2,
        out_specs=vmem,
        scratch_shapes=[
            pltpu.VMEM((n, cap, width), bf16),
            pltpu.VMEM((n, 16, cap), bf16),
            pltpu.VMEM((4, token_rows, width), bf16),
            pltpu.VMEM(base_key_value_weight.shape, bf16),
            pltpu.VMEM(down_factor_pages.shape, bf16),
            pltpu.VMEM((width, wide), bf16),
            pltpu.VMEM((token_rows, columns), f32),
            pltpu.VMEM((4, n, cap, LANES), f32),
            pltpu.VMEM((n, cap, columns), bf16),
            pltpu.VMEM((n, cap, columns), bf16),
            dma((2,)), dma((n,)), dma((n,)), dma((n,)), dma((n,)),
            dma((3,)), dma((3,)), dma((4, n)), dma((4, n)), dma((n,)), dma((n,)),
        ],
        compiler_params=pltpu.CompilerParams(
            collective_id=0, has_side_effects=True, vmem_limit_bytes=52 * 1024 * 1024
        ),
    )(send, which, tokens, combine, up_factor_pages.reshape(wide, columns),
      base_key_value_weight, down_factor_pages)


def solution(mesh):
    return jax.shard_map(
        shards,
        mesh=mesh,
        in_specs=(
            P(("rep", "ad"), "tp"),
            P(("rep", "ad")),
            P("rep"),
            P(None, "tp"),
            P(("rep", "ad"), "tp", None),
            P(("rep", "ad"), None, "tp"),
        ),
        out_specs=P(("rep", "ad"), "tp"),
        check_vma=False,
    )
```

```python
import functools

import jax
import jax.numpy as jnp
from jax import lax
from jax.experimental import pallas as pl
from jax.experimental.pallas import tpu as pltpu
from jax.sharding import PartitionSpec as P

MESH = pl.DeviceIdType.MESH
LANES = 128
DEPTH = 512
PIECES = 4


def kernel(
    n, pieces, rank, disp_ref, which_ref, tok_ref, comb_ref, up_ref, w_hbm, down_hbm, out_ref,
    send, recv, rwhich, gath, w, down, acc, part, dsend, ret,
    local_sem, row_send, row_recv, which_send, which_recv,
    tok_send, tok_recv, part_send, part_recv, ret_send, ret_recv,
):
    me, t = lax.axis_index("ad"), lax.axis_index("tp")
    sibling = t + 1 - 2 * lax.rem(t, 2)
    across = lax.rem(t + 2, 4)
    diagonal = lax.rem(sibling + 2, 4)
    width, wide, cap = tok_ref.shape[1], down.shape[0], which_ref.shape[2]
    h = cap // pieces
    rows = n * h

    barrier = pltpu.get_barrier_semaphore()

    @pl.loop(1, n)
    def _(s):
        pl.semaphore_signal(barrier, inc=1, device_id={"ad": lax.rem(me + s, n)}, device_id_type=MESH)

    for s in range(1, 4):
        pl.semaphore_signal(barrier, inc=1, device_id={"tp": lax.rem(t + s, 4)}, device_id_type=MESH)
    down_copy = pltpu.make_async_copy(down_hbm, down, local_sem.at[0])
    w_copy = pltpu.make_async_copy(w_hbm, w, local_sem.at[1])
    down_copy.start()
    w_copy.start()

    def pack(c):
        send[c] = jnp.dot(
            disp_ref[c], tok_ref[...], preferred_element_type=jnp.float32
        ).astype(jnp.bfloat16).reshape(n, h, width)
        recv[c, me] = send[c, me]

    pack(0)
    rwhich[me] = which_ref[me]
    pl.semaphore_wait(barrier, n - 1 + 3)

    def rows_copy(c, j, slot):
        return pltpu.make_async_remote_copy(
            src_ref=send.at[c, j], dst_ref=recv.at[c, slot], send_sem=row_send.at[c, j],
            recv_sem=row_recv.at[c, slot], device_id={"ad": j}, device_id_type=MESH)

    def which_copy(j, slot):
        return pltpu.make_async_remote_copy(
            src_ref=which_ref.at[j], dst_ref=rwhich.at[slot], send_sem=which_send.at[j],
            recv_sem=which_recv.at[slot], device_id={"ad": j}, device_id_type=MESH)

    def token_copy(k, src, slot, to):
        return pltpu.make_async_remote_copy(
            src_ref=src, dst_ref=gath.at[slot], send_sem=tok_send.at[k],
            recv_sem=tok_recv.at[k], device_id={"tp": to}, device_id_type=MESH)

    def part_copy(c, k, slot, to):
        return pltpu.make_async_remote_copy(
            src_ref=part.at[t, c], dst_ref=part.at[slot, c], send_sem=part_send.at[k, c],
            recv_sem=part_recv.at[slot, c], device_id={"tp": to}, device_id_type=MESH)

    def ret_copy(c, j, slot):
        return pltpu.make_async_remote_copy(
            src_ref=dsend.at[c, j], dst_ref=ret.at[c, slot], send_sem=ret_send.at[c, j],
            recv_sem=ret_recv.at[c, slot], device_id={"ad": j}, device_id_type=MESH)

    def dispatch(c):
        @pl.loop(1, n)
        def _(s):
            j = lax.rem(me + s, n)
            if c == 0:
                which_copy(j, me).start()
            rows_copy(c, j, me).start()

    dispatch(0)
    token_copy(1, tok_ref, t, across).start()
    token_copy(0, tok_ref, t, sibling).start()
    for c in range(1, pieces):
        pack(c)
        dispatch(c)

    lane_page = (lax.broadcasted_iota(jnp.int32, (rows, wide), 1) // rank).astype(jnp.float32)
    own_lane = lax.broadcasted_iota(jnp.int32, (rows, cap), 1) - lax.rem(
        lax.broadcasted_iota(jnp.int32, (rows, cap), 0), h)

    def page_mask(c):
        lines = jnp.concatenate(
            [jnp.broadcast_to(rwhich[j][0:1, :].astype(jnp.float32), (h, cap)) for j in range(n)], axis=0)
        spread = jnp.where(own_lane == c * h, lines, 0.0).astype(jnp.bfloat16)
        column = jnp.dot(spread, jnp.ones((cap, wide), jnp.bfloat16), preferred_element_type=jnp.float32)
        return column == lane_page

    def partial(c):
        @pl.loop(1, n)
        def _(s):
            j = lax.rem(me + s, n)
            if c == 0:
                which_copy(j, j).wait_recv()
            rows_copy(c, j, j).wait_recv()

        first = lax.dot_general(
            recv[c].reshape(rows, width), down[...], (((1,), (1,)), ((), ())),
            preferred_element_type=jnp.float32)
        first = jnp.where(page_mask(c), first, 0.0)
        total = first[:, :LANES]
        for k in range(1, wide // LANES):
            total = total + first[:, k * LANES : (k + 1) * LANES]
        part[t, c] = total
        for k in range(1, 4):
            part_copy(c, k, t, lax.rem(t + k, 4)).start()

    def update(c):
        for k in range(1, 4):
            slot = lax.rem(t + 4 - k, 4)
            part_copy(c, k, slot, slot).wait_recv()
        shrink = part[0, c] + part[1, c] + part[2, c] + part[3, c]
        spread = jnp.concatenate([shrink] * (wide // LANES), axis=1)
        spread = jnp.where(page_mask(c), spread, 0.0).astype(jnp.bfloat16)
        delta = jnp.dot(spread, up_ref[...], preferred_element_type=jnp.float32).astype(jnp.bfloat16)
        dsend[c] = delta.reshape(n, h, delta.shape[1])
        ret[c, me] = dsend[c, me]

        @pl.loop(1, n)
        def _(s):
            ret_copy(c, lax.rem(me + s, n), me).start()

    acc[...] = jnp.zeros_like(acc)
    w_copy.wait()

    def add_base(block, owner):
        @pl.loop(0, width // DEPTH)
        def _(i):
            at = pl.multiple_of(i * DEPTH, DEPTH)
            row = pl.multiple_of(owner * width + i * DEPTH, DEPTH)
            acc[...] += jnp.dot(
                block[:, pl.ds(at, DEPTH)], w[pl.ds(row, DEPTH), :], preferred_element_type=jnp.float32)

    def base_across():
        token_copy(1, tok_ref, across, across).wait_recv()
        token_copy(2, gath.at[across], across, sibling).start()
        add_base(gath.at[across], across)

    def base_diagonal():
        token_copy(2, gath.at[across], diagonal, sibling).wait_recv()
        add_base(gath.at[diagonal], diagonal)

    add_base(tok_ref, t)
    token_copy(0, tok_ref, sibling, sibling).wait_recv()
    add_base(gath.at[sibling], sibling)
    down_copy.wait()
    last = pieces - 1
    for c in range(pieces):
        partial(c)
        if c == last // 2:
            base_across()
        if c == last - 1 or last == 0:
            base_diagonal()
        update(c)

    for c in range(pieces):
        @pl.loop(1, n)
        def _(s, c=c):
            j = lax.rem(me + s, n)
            ret_copy(c, j, j).wait_recv()

    back = ret[...].reshape(pieces * rows, out_ref.shape[1])
    change = jnp.dot(comb_ref[...], back, preferred_element_type=jnp.float32)
    out_ref[...] = (acc[...] + change).astype(out_ref.dtype)

    @pl.loop(1, n)
    def _(s):
        j = lax.rem(me + s, n)
        which_copy(j, me).wait_send()
        for c in range(pieces):
            rows_copy(c, j, me).wait_send()
            ret_copy(c, j, me).wait_send()

    for c in range(pieces):
        for k in range(1, 4):
            part_copy(c, k, t, lax.rem(t + k, 4)).wait_send()

    token_copy(0, tok_ref, t, sibling).wait_send()
    token_copy(1, tok_ref, t, across).wait_send()
    token_copy(2, gath.at[across], across, sibling).wait_send()


def shards(
    tokens,
    request_adapter,
    adapter_page_lookup,
    base_key_value_weight,
    down_factor_pages,
    up_factor_pages,
):
    n = lax.axis_size("ad")
    token_rows, width = tokens.shape
    pages, _, rank = down_factor_pages.shape
    columns = base_key_value_weight.shape[1]
    wide = pages * rank
    cap = max(16, min(4 * token_rows // n, token_rows // 2))
    slots = n * cap
    pieces = max(1, min(PIECES, cap // 16))
    h = cap // pieces

    catalog = jnp.arange(adapter_page_lookup.shape[0], dtype=jnp.int32)
    matches = request_adapter[:, None] == catalog[None, :]
    page = jnp.sum(jnp.where(matches, adapter_page_lookup[None, :], 0), axis=1)
    target = page // pages
    within = page % pages
    order = jnp.arange(token_rows, dtype=jnp.int32)
    earlier = (target[:, None] == target[None, :]) & (order[None, :] < order[:, None])
    position = jnp.sum(earlier.astype(jnp.int32), axis=1)
    place = (position // h) * (n * h) + target * h + position % h
    slot = jnp.arange(slots, dtype=jnp.int32)
    dispatch = slot[:, None] == place[None, :]
    combine = (place[:, None] == slot[None, :]).astype(jnp.bfloat16)
    which = jnp.sum(jnp.where(dispatch, within[None, :], 0), axis=1).astype(jnp.bfloat16)
    which = which.reshape(pieces, n, h).transpose(1, 0, 2).reshape(n, 1, cap)
    which = jnp.broadcast_to(which, (n, 16, cap))
    dispatch = dispatch.astype(jnp.bfloat16).reshape(pieces, n * h, token_rows)
    down = jnp.swapaxes(down_factor_pages, 1, 2).reshape(wide, width)

    vmem = pl.BlockSpec(memory_space=pltpu.VMEM)
    hbm = pl.BlockSpec(memory_space=pl.ANY)
    bf16, f32 = jnp.bfloat16, jnp.float32
    dma = pltpu.SemaphoreType.DMA
    return pl.pallas_call(
        functools.partial(kernel, n, pieces, rank),
        out_shape=jax.ShapeDtypeStruct((token_rows, columns), bf16),
        in_specs=[vmem] * 5 + [hbm] * 2,
        out_specs=vmem,
        scratch_shapes=[
            pltpu.VMEM((pieces, n, h, width), bf16),
            pltpu.VMEM((pieces, n, h, width), bf16),
            pltpu.VMEM((n, 16, cap), bf16),
            pltpu.VMEM((4, token_rows, width), bf16),
            pltpu.VMEM(base_key_value_weight.shape, bf16),
            pltpu.VMEM((wide, width), bf16),
            pltpu.VMEM((token_rows, columns), f32),
            pltpu.VMEM((4, pieces, n * h, LANES), f32),
            pltpu.VMEM((pieces, n, h, columns), bf16),
            pltpu.VMEM((pieces, n, h, columns), bf16),
            dma((2,)), dma((pieces, n)), dma((pieces, n)), dma((n,)), dma((n,)),
            dma((3,)), dma((3,)), dma((4, pieces)), dma((4, pieces)),
            dma((pieces, n)), dma((pieces, n)),
        ],
        compiler_params=pltpu.CompilerParams(
            collective_id=0, has_side_effects=True, vmem_limit_bytes=52 * 1024 * 1024
        ),
    )(dispatch, which, tokens, combine, up_factor_pages.reshape(wide, columns),
      base_key_value_weight, down)


def solution(mesh):
    return jax.shard_map(
        shards,
        mesh=mesh,
        in_specs=(
            P(("rep", "ad"), "tp"),
            P(("rep", "ad")),
            P("rep"),
            P(None, "tp"),
            P(("rep", "ad"), "tp", None),
            P(("rep", "ad"), None, "tp"),
        ),
        out_specs=P(("rep", "ad"), "tp"),
        check_vma=False,
    )
```

```python
import functools

import jax
import jax.numpy as jnp
from jax import lax
from jax.experimental import pallas as pl
from jax.experimental.pallas import tpu as pltpu
from jax.sharding import PartitionSpec as P

MESH = pl.DeviceIdType.MESH
LANES = 128
DEPTH = 512
PIECES = 4


def kernel(
    n, pieces, rank, disp_ref, which_ref, tok_ref, comb_ref, up_ref, w_hbm, down_hbm, out_ref,
    send, recv, rwhich, gath, w, down, acc, part, dsend, ret,
    local_sem, row_send, row_recv, which_send, which_recv,
    tok_send, tok_recv, part_send, part_recv, ret_send, ret_recv,
):
    me, t = lax.axis_index("ad"), lax.axis_index("tp")
    sibling = t + 1 - 2 * lax.rem(t, 2)
    across = lax.rem(t + 2, 4)
    diagonal = lax.rem(sibling + 2, 4)
    width, wide, cap = tok_ref.shape[1], down.shape[0], which_ref.shape[2]
    h = cap // pieces
    rows = n * h

    barrier = pltpu.get_barrier_semaphore()

    @pl.loop(1, n)
    def _(s):
        pl.semaphore_signal(barrier, inc=1, device_id={"ad": lax.rem(me + s, n)}, device_id_type=MESH)

    for s in range(1, 4):
        pl.semaphore_signal(barrier, inc=1, device_id={"tp": lax.rem(t + s, 4)}, device_id_type=MESH)
    down_copy = pltpu.make_async_copy(down_hbm, down, local_sem.at[0])
    w_copy = pltpu.make_async_copy(w_hbm, w, local_sem.at[1])
    down_copy.start()
    w_copy.start()

    def pack(c):
        send[c] = jnp.dot(
            disp_ref[c], tok_ref[...], preferred_element_type=jnp.float32
        ).astype(jnp.bfloat16).reshape(n, h, width)
        recv[c, me] = send[c, me]

    pack(0)
    rwhich[me] = which_ref[me]
    pl.semaphore_wait(barrier, n - 1 + 3)

    def rows_copy(c, j, slot):
        return pltpu.make_async_remote_copy(
            src_ref=send.at[c, j], dst_ref=recv.at[c, slot], send_sem=row_send.at[c, j],
            recv_sem=row_recv.at[c, slot], device_id={"ad": j}, device_id_type=MESH)

    def which_copy(j, slot):
        return pltpu.make_async_remote_copy(
            src_ref=which_ref.at[j], dst_ref=rwhich.at[slot], send_sem=which_send.at[j],
            recv_sem=which_recv.at[slot], device_id={"ad": j}, device_id_type=MESH)

    def token_copy(k, src, slot, to):
        return pltpu.make_async_remote_copy(
            src_ref=src, dst_ref=gath.at[slot], send_sem=tok_send.at[k],
            recv_sem=tok_recv.at[k], device_id={"tp": to}, device_id_type=MESH)

    def part_copy(c, k, slot, to):
        return pltpu.make_async_remote_copy(
            src_ref=part.at[t, c], dst_ref=part.at[slot, c], send_sem=part_send.at[k, c],
            recv_sem=part_recv.at[slot, c], device_id={"tp": to}, device_id_type=MESH)

    def ret_copy(c, j, slot):
        return pltpu.make_async_remote_copy(
            src_ref=dsend.at[c, j], dst_ref=ret.at[c, slot], send_sem=ret_send.at[c, j],
            recv_sem=ret_recv.at[c, slot], device_id={"ad": j}, device_id_type=MESH)

    def target(i):
        s = 1 + lax.rem(i + n // 2 + n - 3, n - 1)
        return lax.rem(me + s + lax.rem(me, 2) * (n - 2 * s), n)

    def dispatch(c):
        @pl.loop(1, n)
        def _(s):
            j = target(s)
            if c == 0:
                which_copy(j, me).start()
            rows_copy(c, j, me).start()

    dispatch(0)
    token_copy(1, tok_ref, t, across).start()
    token_copy(0, tok_ref, t, sibling).start()
    for c in range(1, pieces):
        pack(c)
        dispatch(c)

    lane_page = (lax.broadcasted_iota(jnp.int32, (rows, wide), 1) // rank).astype(jnp.float32)
    own_lane = lax.broadcasted_iota(jnp.int32, (rows, cap), 1) - lax.rem(
        lax.broadcasted_iota(jnp.int32, (rows, cap), 0), h)

    def page_mask(c):
        lines = jnp.concatenate(
            [jnp.broadcast_to(rwhich[j][0:1, :].astype(jnp.float32), (h, cap)) for j in range(n)], axis=0)
        spread = jnp.where(own_lane == c * h, lines, 0.0).astype(jnp.bfloat16)
        column = jnp.dot(spread, jnp.ones((cap, wide), jnp.bfloat16), preferred_element_type=jnp.float32)
        return column == lane_page

    def partial(c):
        @pl.loop(1, n)
        def _(s):
            j = lax.rem(me + s, n)
            if c == 0:
                which_copy(j, j).wait_recv()
            rows_copy(c, j, j).wait_recv()

        first = lax.dot_general(
            recv[c].reshape(rows, width), down[...], (((1,), (1,)), ((), ())),
            preferred_element_type=jnp.float32)
        first = jnp.where(page_mask(c), first, 0.0)
        total = first[:, :LANES]
        for k in range(1, wide // LANES):
            total = total + first[:, k * LANES : (k + 1) * LANES]
        part[t, c] = total
        for k in range(1, 4):
            part_copy(c, k, t, lax.rem(t + k, 4)).start()

    def update(c):
        for k in range(1, 4):
            slot = lax.rem(t + 4 - k, 4)
            part_copy(c, k, slot, slot).wait_recv()
        shrink = part[0, c] + part[1, c] + part[2, c] + part[3, c]
        spread = jnp.concatenate([shrink] * (wide // LANES), axis=1)
        spread = jnp.where(page_mask(c), spread, 0.0).astype(jnp.bfloat16)
        delta = jnp.dot(spread, up_ref[...], preferred_element_type=jnp.float32).astype(jnp.bfloat16)
        dsend[c] = delta.reshape(n, h, delta.shape[1])
        ret[c, me] = dsend[c, me]

        @pl.loop(1, n)
        def _(s):
            ret_copy(c, target(s), me).start()

    acc[...] = jnp.zeros_like(acc)
    w_copy.wait()

    def add_base(block, owner):
        @pl.loop(0, width // DEPTH)
        def _(i):
            at = pl.multiple_of(i * DEPTH, DEPTH)
            row = pl.multiple_of(owner * width + i * DEPTH, DEPTH)
            acc[...] += jnp.dot(
                block[:, pl.ds(at, DEPTH)], w[pl.ds(row, DEPTH), :], preferred_element_type=jnp.float32)

    def base_across():
        token_copy(1, tok_ref, across, across).wait_recv()
        token_copy(2, gath.at[across], across, sibling).start()
        add_base(gath.at[across], across)

    def base_diagonal():
        token_copy(2, gath.at[across], diagonal, sibling).wait_recv()
        add_base(gath.at[diagonal], diagonal)

    add_base(tok_ref, t)
    token_copy(0, tok_ref, sibling, sibling).wait_recv()
    add_base(gath.at[sibling], sibling)
    down_copy.wait()
    last = pieces - 1
    for c in range(pieces):
        partial(c)
        if c == last // 2:
            base_across()
        if c == last - 1 or last == 0:
            base_diagonal()
        update(c)

    for c in range(pieces):
        @pl.loop(1, n)
        def _(s, c=c):
            j = lax.rem(me + s, n)
            ret_copy(c, j, j).wait_recv()

    back = ret[...].reshape(pieces * rows, out_ref.shape[1])
    change = jnp.dot(comb_ref[...], back, preferred_element_type=jnp.float32)
    out_ref[...] = (acc[...] + change).astype(out_ref.dtype)

    @pl.loop(1, n)
    def _(s):
        j = lax.rem(me + s, n)
        which_copy(j, me).wait_send()
        for c in range(pieces):
            rows_copy(c, j, me).wait_send()
            ret_copy(c, j, me).wait_send()

    for c in range(pieces):
        for k in range(1, 4):
            part_copy(c, k, t, lax.rem(t + k, 4)).wait_send()

    token_copy(0, tok_ref, t, sibling).wait_send()
    token_copy(1, tok_ref, t, across).wait_send()
    token_copy(2, gath.at[across], across, sibling).wait_send()


def shards(
    tokens,
    request_adapter,
    adapter_page_lookup,
    base_key_value_weight,
    down_factor_pages,
    up_factor_pages,
):
    n = lax.axis_size("ad")
    token_rows, width = tokens.shape
    pages, _, rank = down_factor_pages.shape
    columns = base_key_value_weight.shape[1]
    wide = pages * rank
    cap = max(16, min(4 * token_rows // n, token_rows // 2))
    slots = n * cap
    pieces = max(1, min(PIECES, cap // 16))
    h = cap // pieces

    catalog = jnp.arange(adapter_page_lookup.shape[0], dtype=jnp.int32)
    matches = request_adapter[:, None] == catalog[None, :]
    page = jnp.sum(jnp.where(matches, adapter_page_lookup[None, :], 0), axis=1)
    target = page // pages
    within = page % pages
    order = jnp.arange(token_rows, dtype=jnp.int32)
    earlier = (target[:, None] == target[None, :]) & (order[None, :] < order[:, None])
    position = jnp.sum(earlier.astype(jnp.int32), axis=1)
    place = (position // h) * (n * h) + target * h + position % h
    slot = jnp.arange(slots, dtype=jnp.int32)
    dispatch = slot[:, None] == place[None, :]
    combine = (place[:, None] == slot[None, :]).astype(jnp.bfloat16)
    which = jnp.sum(jnp.where(dispatch, within[None, :], 0), axis=1).astype(jnp.bfloat16)
    which = which.reshape(pieces, n, h).transpose(1, 0, 2).reshape(n, 1, cap)
    which = jnp.broadcast_to(which, (n, 16, cap))
    dispatch = dispatch.astype(jnp.bfloat16).reshape(pieces, n * h, token_rows)
    down = jnp.swapaxes(down_factor_pages, 1, 2).reshape(wide, width)

    vmem = pl.BlockSpec(memory_space=pltpu.VMEM)
    hbm = pl.BlockSpec(memory_space=pl.ANY)
    bf16, f32 = jnp.bfloat16, jnp.float32
    dma = pltpu.SemaphoreType.DMA
    return pl.pallas_call(
        functools.partial(kernel, n, pieces, rank),
        out_shape=jax.ShapeDtypeStruct((token_rows, columns), bf16),
        in_specs=[vmem] * 5 + [hbm] * 2,
        out_specs=vmem,
        scratch_shapes=[
            pltpu.VMEM((pieces, n, h, width), bf16),
            pltpu.VMEM((pieces, n, h, width), bf16),
            pltpu.VMEM((n, 16, cap), bf16),
            pltpu.VMEM((4, token_rows, width), bf16),
            pltpu.VMEM(base_key_value_weight.shape, bf16),
            pltpu.VMEM((wide, width), bf16),
            pltpu.VMEM((token_rows, columns), f32),
            pltpu.VMEM((4, pieces, n * h, LANES), f32),
            pltpu.VMEM((pieces, n, h, columns), bf16),
            pltpu.VMEM((pieces, n, h, columns), bf16),
            dma((2,)), dma((pieces, n)), dma((pieces, n)), dma((n,)), dma((n,)),
            dma((3,)), dma((3,)), dma((4, pieces)), dma((4, pieces)),
            dma((pieces, n)), dma((pieces, n)),
        ],
        compiler_params=pltpu.CompilerParams(
            collective_id=0, has_side_effects=True, vmem_limit_bytes=52 * 1024 * 1024
        ),
    )(dispatch, which, tokens, combine, up_factor_pages.reshape(wide, columns),
      base_key_value_weight, down)


def solution(mesh):
    return jax.shard_map(
        shards,
        mesh=mesh,
        in_specs=(
            P(("rep", "ad"), "tp"),
            P(("rep", "ad")),
            P("rep"),
            P(None, "tp"),
            P(("rep", "ad"), "tp", None),
            P(("rep", "ad"), None, "tp"),
        ),
        out_specs=P(("rep", "ad"), "tp"),
        check_vma=False,
    )
```
